32 devices in a mesh: row: 4 (over z), col: 8 (over y, x, core).
Axes of the slice: x: 2, y: 2, z: 4, core: 2. Of those that a mesh axis runs over, the one named last changes fastest.
Arguments:
- tokens: bfloat16 [2048, 2048], P('col', 'row'), may hold values from -6 to 6
- router: bfloat16 [2048, 16], replicated, may hold values from -0.125 to 0.125
- shared_gate_vector: bfloat16 [2048], replicated, may hold values from -0.125 to 0.125
- shared_gate_weight: bfloat16 [2048, 5632], P('col', 'row'), may hold values from -0.125 to 0.125
- shared_up_weight: bfloat16 [2048, 5632], P('col', 'row'), may hold values from -0.125 to 0.125
- shared_down_weight: bfloat16 [5632, 2048], P('row', 'col'), may hold values from -0.078125 to 0.078125
- routed_gate_weight: bfloat16 [16, 2048, 1408], P('col', None, 'row'), may hold values from -0.125 to 0.125
- routed_up_weight: bfloat16 [16, 2048, 1408], P('col', None, 'row'), may hold values from -0.125 to 0.125
- routed_down_weight: bfloat16 [16, 1408, 2048], P('col', 'row'), may hold values from -0.15625 to 0.15625
- adapter_input_factor: bfloat16 [64, 16, 2048], P(None, None, 'row'), may hold values from -0.125 to 0.125
- adapter_output_factor: bfloat16 [64, 16, 5632], P(None, None, 'row'), may hold values from -0.29882812 to 0.29882812
- routes: int32 [2048, 4], P('col'), may hold values from 0 to 15, all different within a row; in each aligned block of 256 rows (0 to 255, 256 to 511, ...) at most 128 rows name the same one
- lengths: int32 [8, 16], P('col'), may hold values from 1 to 128, 256 in all within a row
- prompt_adapter_index: int32 [8, 16], P('col'), may hold values from 0 to 15
- active_adapter_index: int32 [16], replicated, may hold values from 0 to 63, as said below
Outputs:
- moe_out: float32 [2048, 2048], P('col', 'row')
The draws below stay inside these ranges and needn't reach their ends.
Inputs may be any that keep to these rules, and one draw needn't show every extreme that they name: `routes`: in each group of 256 consecutive tokens no expert is named by more than 128 tokens, a bound that some block reaches. Each group's 16 lengths sum to 256; the longest is exactly 128. `active_adapter_index`: the 16 entries are distinct.
All inputs are finite; a program needn't handle non-finite values.
Results may differ from the reference program's by a relative error of at most 0.003.
Values may be sent and summed in bfloat16 or wider, within the bound.
A program may use at most 128 MiB of HBM per device.

```python
import math
import jax
import jax.numpy as jnp
import numpy as np
from jax import lax

MODEL_WIDTH = 2048
FF = 1408
SHARED_UNITS = 5632
TOP = 4
ADAPTER_RANK = 16
ADAPTER_COUNT = 64
NACT = 16
TOK_DEV = 256
NREQ = 16
PROMPT_MAX = 128
GROUPS = 8
TOKENS = 2048
EXPERTS = 16
CAP = 128
N_COL = 8


def draw_active_adapter_index(key, part):
    order = jax.random.permutation(key, ADAPTER_COUNT)
    return order[:NACT].astype(jnp.int32)


def plant(drawn, own_key, low, top_value):
    longest = drawn.shape.index(max(drawn.shape))
    spots = []
    for shift in (0, 1):
        where = [jax.random.randint(jax.random.fold_in(own_key, axis), (), 0, length) for axis, length in enumerate(drawn.shape)]
        where[longest] = (where[longest] + shift) % drawn.shape[longest]
        spots.append(tuple(where))
    return drawn.at[spots[0]].set(low).at[spots[1]].set(top_value)


def block_levels(rng, dims, cuts, low, top_value):
    factor_of = 1.0
    for dim, shards_of in cuts:
        heights = jax.random.uniform(jax.random.fold_in(jax.random.fold_in(rng, 6), dim), (shards_of,), jnp.float32, low / len(cuts), top_value / len(cuts))
        factor_of = factor_of * jnp.repeat(jnp.exp(heights), dims[dim] // shards_of).reshape((-1,) + (1,) * (len(dims) - 1 - dim))
    return factor_of


def length_profile(amount, total, most, lean):
    weights = [(1 << 20) // math.isqrt(standing ** lean) + 1 for standing in range(2, amount + 1)]
    spare, counts = total - most - (amount - 1), [1] * (amount - 1)
    while spare > 0:
        free = [i for i in range(amount - 1) if counts[i] < most]
        whole, remaining = sum([weights[i] for i in free]), spare
        for i in free:
            more = min(most - counts[i], max(1, remaining * weights[i] // whole), spare)
            counts[i] = counts[i] + more
            spare = spare - more
    return np.array([most] + counts)


def ragged(own_key, number_of, total, reach, slope):
    if number_of == 2:
        one = jax.random.randint(own_key, (), max(1, total - reach), min(reach, total - 1) + 1)
        return jnp.stack([one, total - one])
    sizes = jnp.asarray(length_profile(number_of, total, reach, slope), jnp.int32)
    couples = (number_of - 1) // 2
    giver, taker = sizes[1:1 + 2 * couples:2], sizes[2:2 + 2 * couples:2]
    margin = jnp.minimum(giver - 1, reach - taker)
    shifted = jax.random.randint(jax.random.fold_in(own_key, 1), (couples,), 0, 1 << 20) % (margin + 1)
    sizes = sizes.at[1:1 + 2 * couples:2].set(giver - shifted).at[2:2 + 2 * couples:2].set(taker + shifted)
    return sizes[jax.random.permutation(jax.random.fold_in(own_key, 2), number_of)]


def deal_out(own_key, own, number, rows, count, top, limit, lean):
    ranking = jax.random.permutation(own_key, count)
    crowded, common = shares(count, rows * top, limit, lean, True), shares(count, rows * top, limit, lean, False)
    places = jnp.arange(count)

    def named(tallies, turn):
        used = int((tallies > 0).sum())
        fixed = max(1, used // 4)
        passed = fixed + (places - fixed + turn * (used - fixed)) % max(1, count - fixed)
        return jnp.zeros((count,), jnp.int32).at[ranking[jnp.where(places < fixed, places, passed)]].set(jnp.asarray(tallies, jnp.int32))

    tallies = jnp.where(number % 4 == 0, named(crowded, number // 4), named(common, number - number // 4 - 1))
    mixed = jax.random.permutation(jax.random.fold_in(own, 3), count)
    donor, receiver = mixed[0:count // 2 * 2:2], mixed[1:count // 2 * 2:2]
    margin = jnp.minimum(tallies[donor] - 1, limit - tallies[receiver]) // 2
    margin = jnp.where((donor == ranking[0]) | (receiver == ranking[0]) | (tallies[receiver] == 0), 0, jnp.maximum(margin, 0))
    passed = jax.random.randint(jax.random.fold_in(own, 4), (count // 2,), 0, 1 << 20) % (margin + 1)
    tallies = tallies.at[donor].add(-passed).at[receiver].add(passed)
    items = jnp.searchsorted(jnp.cumsum(tallies), jnp.arange(rows * top), side="right").astype(jnp.int32)
    grid = items.reshape(top, rows).T
    grid = grid[jax.random.permutation(jax.random.fold_in(own, 1), rows)]
    turn = jax.random.randint(jax.random.fold_in(own, 2), (rows, 1), 0, top)
    return jnp.take_along_axis(grid, (jnp.arange(top)[None, :] + turn) % top, axis=1)


def shares(amount, total, most, slope, full):
    weights = [(1 << 20) // math.isqrt(grade ** slope) + 1 for grade in range(1, amount + 1)]
    largest = most if full else min(most, max(-(-total // amount), total * weights[0] // sum(weights)))
    least = 1 if total - largest >= amount - 1 else 0
    holding, surplus = [largest] + [least] * (amount - 1), total - largest - least * (amount - 1)
    while surplus > 0:
        movable = [i for i in range(1, amount) if holding[i] < largest] or [i for i in range(1, amount) if holding[i] < most]
        whole, remaining = sum([weights[i] for i in movable]), surplus
        for i in movable:
            addition = min(most - holding[i], max(1, remaining * weights[i] // whole), surplus)
            holding[i] = holding[i] + addition
            surplus = surplus - addition
    return np.array(holding)


def scatter_about(key, extent, spread, bound, shards=(), kind=jnp.bfloat16):
    result = spread * jax.random.normal(key, extent, jnp.float32)
    if shards:
        result = result * block_levels(key, extent, shards, -0.22, 0.18)
    return jnp.clip(result, -bound, bound).astype(kind)


def setup_inputs(seed: int = 0) -> dict:
    arg_keys = jax.random.split(jax.random.key(seed), 16)
    tokens = scatter_about(arg_keys[0], (TOKENS, MODEL_WIDTH), 1.0, 6.0, ((0, 8), (1, 4)))
    router = scatter_about(arg_keys[1], (MODEL_WIDTH, EXPERTS), MODEL_WIDTH ** -0.5, 0.125)
    shared_gate_vector = scatter_about(arg_keys[2], (MODEL_WIDTH,), MODEL_WIDTH ** -0.5, 0.125)
    shared_gate_weight = scatter_about(arg_keys[3], (MODEL_WIDTH, SHARED_UNITS), MODEL_WIDTH ** -0.5, 0.125, ((0, 8), (1, 4)))
    shared_up_weight = scatter_about(arg_keys[4], (MODEL_WIDTH, SHARED_UNITS), MODEL_WIDTH ** -0.5, 0.125, ((0, 8), (1, 4)))
    shared_down_weight = scatter_about(arg_keys[5], (SHARED_UNITS, MODEL_WIDTH), SHARED_UNITS ** -0.5, 0.078125, ((0, 4), (1, 8)))
    routed_gate_weight = scatter_about(arg_keys[6], (EXPERTS, MODEL_WIDTH, FF), MODEL_WIDTH ** -0.5, 0.125, ((0, 8), (2, 4)))
    routed_up_weight = scatter_about(arg_keys[7], (EXPERTS, MODEL_WIDTH, FF), MODEL_WIDTH ** -0.5, 0.125, ((0, 8), (2, 4)))
    routed_down_weight = scatter_about(arg_keys[8], (EXPERTS, FF, MODEL_WIDTH), FF ** -0.5, 0.15625, ((0, 8), (1, 4)))
    adapter_input_factor = scatter_about(arg_keys[9], (ADAPTER_COUNT, ADAPTER_RANK, MODEL_WIDTH), MODEL_WIDTH ** -0.5, 0.125, ((2, 4),))
    adapter_output_factor = scatter_about(arg_keys[10], (ADAPTER_COUNT, ADAPTER_RANK, SHARED_UNITS), 0.05, 0.29882812, ((2, 4),))
    routes_keys = jax.random.split(jax.random.fold_in(arg_keys[11], 1), TOKENS // TOK_DEV)
    routes_turns = jax.random.permutation(jax.random.fold_in(arg_keys[11], 3), TOKENS // TOK_DEV)
    routes = jax.vmap(lambda own, number: deal_out(jax.random.fold_in(arg_keys[11], 2), own, number, TOK_DEV, EXPERTS, TOP, CAP, 2))(routes_keys, routes_turns).reshape((TOKENS, TOP))
    lengths = jax.vmap(lambda own: ragged(own, NREQ, TOK_DEV, PROMPT_MAX, 2))(jax.random.split(arg_keys[12], GROUPS)).reshape((GROUPS, NREQ)).astype(jnp.int32)
    prompt_adapter_index = plant(jax.random.randint(arg_keys[13], (GROUPS, NREQ), 0, NACT), jax.random.fold_in(arg_keys[13], 1), 0, NACT - 1).astype(jnp.int32)
    active_adapter_index = draw_active_adapter_index(jax.random.fold_in(arg_keys[15], 71), 0)
    return {"tokens": tokens, "router": router, "shared_gate_vector": shared_gate_vector, "shared_gate_weight": shared_gate_weight, "shared_up_weight": shared_up_weight, "shared_down_weight": shared_down_weight, "routed_gate_weight": routed_gate_weight, "routed_up_weight": routed_up_weight, "routed_down_weight": routed_down_weight, "adapter_input_factor": adapter_input_factor, "adapter_output_factor": adapter_output_factor, "routes": routes, "lengths": lengths, "prompt_adapter_index": prompt_adapter_index, "active_adapter_index": active_adapter_index}


ADAPTER_SCALE = 2.0


def reference(tokens, router, shared_gate_vector, shared_gate_weight, shared_up_weight, shared_down_weight, routed_gate_weight, routed_up_weight, routed_down_weight, adapter_input_factor, adapter_output_factor, routes, lengths, prompt_adapter_index, active_adapter_index):
    logits = jnp.dot(tokens, router, preferred_element_type=jnp.float32)
    picked = jnp.take_along_axis(logits, routes, axis=1)
    raw_exp = jnp.exp(picked)
    gate_weights = raw_exp / jnp.sum(raw_exp, axis=1, keepdims=True)
    share = jax.nn.sigmoid(jnp.dot(tokens, shared_gate_vector, preferred_element_type=jnp.float32))

    request_ends = jnp.cumsum(lengths, axis=1).astype(jnp.int32)
    position = jnp.arange(TOK_DEV, dtype=jnp.int32)
    request_of = jnp.sum((position[None, :, None] >= request_ends[:, None, :]).astype(jnp.int32), axis=2).astype(jnp.int32)
    slot_of = jnp.take_along_axis(prompt_adapter_index, request_of, axis=1).reshape(TOKENS)
    reduced_rank_value = NACT * ADAPTER_RANK
    picked_input_factor = jnp.take(adapter_input_factor, active_adapter_index, axis=0).reshape(reduced_rank_value, MODEL_WIDTH)
    picked_output_factor = jnp.take(adapter_output_factor, active_adapter_index, axis=0).reshape(reduced_rank_value, SHARED_UNITS)
    low_rank = lax.dot_general(tokens, picked_input_factor, (((1,), (1,)), ((), ())), preferred_element_type=jnp.float32).astype(jnp.bfloat16)
    owner = (jnp.arange(reduced_rank_value, dtype=jnp.int32) // ADAPTER_RANK).astype(jnp.int32)
    adapter_mask = slot_of[:, None] == owner[None, :]
    low_masked = jnp.where(adapter_mask, low_rank, jnp.zeros((), jnp.bfloat16))
    adapter_update = jnp.dot(low_masked, picked_output_factor, preferred_element_type=jnp.float32)
    shared_gate_value = jnp.dot(tokens, shared_gate_weight, preferred_element_type=jnp.float32)
    shared_up_value = jnp.dot(tokens, shared_up_weight, preferred_element_type=jnp.float32) + ADAPTER_SCALE * adapter_update
    shared_hidden_units = (jax.nn.silu(shared_gate_value) * shared_up_value).astype(jnp.bfloat16)
    shared_out = jnp.dot(shared_hidden_units, shared_down_weight, preferred_element_type=jnp.float32)

    slots_all = N_COL * CAP
    slot_index = jnp.arange(slots_all, dtype=jnp.int32)

    def run_expert(packed):
        weights_gate, weights_up, weights_down, expert_id = packed
        hit_flags = jnp.any(routes == expert_id, axis=1).astype(jnp.int32)
        running = jnp.cumsum(hit_flags).astype(jnp.int32)
        slot_token = jnp.sum((running[None, :] <= slot_index[:, None]).astype(jnp.int32), axis=1).astype(jnp.int32)
        slot_valid = slot_index < running[-1]
        gathered = jnp.take(tokens, jnp.minimum(slot_token, TOKENS - 1), axis=0)
        gathered = jnp.where(slot_valid[:, None], gathered, jnp.zeros((), jnp.bfloat16))
        gate_part = jnp.dot(gathered, weights_gate, preferred_element_type=jnp.float32)
        up_part = jnp.dot(gathered, weights_up, preferred_element_type=jnp.float32)
        hidden = (jax.nn.silu(gate_part) * up_part).astype(jnp.bfloat16)
        return jnp.dot(hidden, weights_down, preferred_element_type=jnp.float32)

    expert_rows = lax.map(run_expert, (routed_gate_weight, routed_up_weight, routed_down_weight, jnp.arange(EXPERTS, dtype=jnp.int32)))
    onehot = routes[:, :, None] == jnp.arange(EXPERTS, dtype=jnp.int32)[None, None, :]
    hit_table = jnp.any(onehot, axis=1).astype(jnp.int32)
    slot_rank = (jnp.cumsum(hit_table, axis=0) - hit_table).astype(jnp.int32)
    route_rank = jnp.sum(jnp.where(onehot, slot_rank[:, None, :], 0), axis=2).astype(jnp.int32)
    row_index = (routes * slots_all + route_rank).astype(jnp.int32)
    routed_rows = jnp.take(expert_rows.reshape(EXPERTS * slots_all, MODEL_WIDTH), row_index, axis=0)
    routed = jnp.sum(gate_weights[:, :, None] * routed_rows, axis=1)
    return routed + share[:, None] * shared_out
```

```python
import jax
import jax.numpy as jnp
from jax import lax
from jax.sharding import PartitionSpec as P

ADAPTER_SCALE = 2.0
BF = jnp.bfloat16
F32 = jnp.float32


def dot(a, b):
    return jnp.dot(a, b, preferred_element_type=F32)


def on_device(
    tokens,
    router,
    shared_gate_vector,
    shared_gate_weight,
    shared_up_weight,
    shared_down_weight,
    routed_gate_weight,
    routed_up_weight,
    routed_down_weight,
    adapter_input_factor,
    adapter_output_factor,
    routes,
    lengths,
    prompt_adapter_index,
    active_adapter_index,
):
    token_count, local_width = tokens.shape
    col_count = lax.axis_size("col")
    col = lax.axis_index("col")
    local_experts = routed_gate_weight.shape[0]
    expert_count = local_experts * col_count
    route_count = routes.shape[1]
    capacity = 2 * token_count * route_count // expert_count
    adapter_count, rank, _ = adapter_input_factor.shape
    request_count = lengths.shape[1]

    all_features = lax.all_gather(tokens, "row", axis=1, tiled=True)
    full_width = all_features.shape[1]
    all_routes = lax.all_gather(routes, "col", axis=0, tiled=False)
    all_tokens = lax.all_gather(all_features, "col", axis=0, tiled=False)
    gate_full = lax.all_gather(shared_gate_weight, "col", axis=0, tiled=True)
    up_full = lax.all_gather(shared_up_weight, "col", axis=0, tiled=True)
    down_full = lax.all_gather(shared_down_weight, "col", axis=1, tiled=True)

    steps = jnp.arange(request_count, dtype=jnp.int32)
    ends = jnp.sum(jnp.where(steps[:, None] <= steps[None, :], lengths[0][:, None], 0), axis=0)
    position = jnp.arange(token_count, dtype=jnp.int32)
    request_of = jnp.sum((position[:, None] >= ends[None, :]).astype(jnp.int32), axis=1)
    adapter_of_request = jnp.sum(
        jnp.where(
            prompt_adapter_index[0][:, None] == jnp.arange(active_adapter_index.shape[0])[None, :],
            active_adapter_index[None, :],
            0,
        ),
        axis=1,
    )
    adapter_of = jnp.sum(
        jnp.where(request_of[:, None] == steps[None, :], adapter_of_request[None, :], 0), axis=1
    )
    owner = jnp.arange(adapter_count * rank, dtype=jnp.int32) // rank
    mask = adapter_of[:, None] == owner[None, :]
    low_part = lax.dot_general(
        tokens,
        adapter_input_factor.reshape(adapter_count * rank, local_width),
        (((1,), (1,)), ((), ())),
        preferred_element_type=F32,
    )
    low_own = jnp.sum(
        jnp.where(mask, low_part, 0.0).reshape(token_count, adapter_count, rank), axis=1
    )
    low = lax.psum(low_own, "row").astype(BF)
    low_masked = jnp.where(mask, jnp.tile(low, (1, adapter_count)), jnp.zeros((), BF))
    delta = dot(
        low_masked, adapter_output_factor.reshape(adapter_count * rank, adapter_output_factor.shape[2])
    )

    logits = dot(all_features, router)
    experts = jnp.arange(expert_count, dtype=jnp.int32)
    onehot = routes[:, :, None] == experts[None, None, :]
    picked = jnp.sum(jnp.where(onehot, logits[:, None, :], 0.0), axis=2)
    raw_exp = jnp.exp(picked)
    gate_weights = raw_exp / jnp.sum(raw_exp, axis=1, keepdims=True)
    share = jax.nn.sigmoid(dot(all_features, shared_gate_vector))
    tri = (position[None, :] < position[:, None]).astype(BF)
    hit = jnp.any(onehot, axis=1)
    rank_own = dot(tri, hit.astype(BF)).astype(jnp.int32)
    weight_of = jnp.sum(jnp.where(onehot, gate_weights[:, :, None], 0.0), axis=1)
    slots = jnp.arange(capacity, dtype=jnp.int32)
    here = hit[:, :, None] & (rank_own[:, :, None] == slots[None, None, :])
    combine = jnp.where(here, weight_of[:, :, None], 0.0).reshape(token_count, expert_count * capacity)
    combine_hi = combine.astype(BF)
    combine_lo = (combine - combine_hi.astype(F32)).astype(BF)

    own_experts = col * local_experts + jnp.arange(local_experts, dtype=jnp.int32)
    hit_all = jnp.any(all_routes[:, :, :, None] == own_experts[None, None, None, :], axis=2)
    rank_all = jnp.einsum(
        "ts,gse->gte", tri, hit_all.astype(BF), preferred_element_type=F32
    ).astype(jnp.int32)
    pick = (
        (hit_all[:, :, :, None] & (rank_all[:, :, :, None] == slots[None, None, None, :]))
        .astype(BF)
        .transpose(2, 0, 3, 1)
    )
    rows = jnp.einsum("egst,gtd->egsd", pick, all_tokens, preferred_element_type=F32).astype(BF)
    rows = rows.reshape(local_experts, col_count * capacity, full_width)
    gate_part = jnp.einsum("esd,edf->esf", rows, routed_gate_weight, preferred_element_type=F32)
    up_part = jnp.einsum("esd,edf->esf", rows, routed_up_weight, preferred_element_type=F32)
    hidden = (jax.nn.silu(gate_part) * up_part).astype(BF)
    partial = jnp.einsum(
        "esf,efd->esd", hidden, routed_down_weight, preferred_element_type=F32
    ).astype(BF)
    outgoing = partial.reshape(local_experts, col_count, capacity, full_width).transpose(1, 0, 2, 3)
    returned = lax.all_to_all(outgoing, "col", split_axis=0, concat_axis=0, tiled=True)
    flat = returned.reshape(expert_count * capacity, full_width)

    shared_gate_value = dot(all_features, gate_full)
    shared_up_value = dot(all_features, up_full)
    shared_hidden = (
        jax.nn.silu(shared_gate_value) * (shared_up_value + ADAPTER_SCALE * delta)
    ).astype(BF)
    shared_part = dot(shared_hidden, down_full) * share[:, None]

    total = dot(combine_hi, flat) + dot(combine_lo, flat) + shared_part
    return lax.psum_scatter(total, "row", scatter_dimension=1, tiled=True)


def solution(mesh):
    return jax.shard_map(
        on_device,
        mesh=mesh,
        in_specs=(
            P("col", "row"),
            P(),
            P(),
            P("col", "row"),
            P("col", "row"),
            P("row", "col"),
            P("col", None, "row"),
            P("col", None, "row"),
            P("col", "row", None),
            P(None, None, "row"),
            P(None, None, "row"),
            P("col", None),
            P("col", None),
            P("col", None),
            P(),
        ),
        out_specs=P("col", "row"),
        check_vma=False,
    )
```

```python
import functools

import jax
import jax.numpy as jnp
from jax import lax
from jax.experimental import pallas as pl
from jax.experimental.pallas import tpu as pltpu
from jax.sharding import PartitionSpec as P

ADAPTER_SCALE = 2.0
BF = jnp.bfloat16
F32 = jnp.float32


def dot(a, b):
    return jnp.dot(a, b, preferred_element_type=F32)


def remote(src, dst, send, recv, row, col):
    return pltpu.make_async_remote_copy(
        src_ref=src,
        dst_ref=dst,
        send_sem=send,
        recv_sem=recv,
        device_id=(row, col),
        device_id_type=pl.DeviceIdType.MESH,
    )


def greet(nrow, ncol, row, col):
    barrier = pltpu.get_barrier_semaphore()
    for k in range(1, nrow):
        pl.semaphore_signal(
            barrier,
            inc=1,
            device_id=(lax.rem(row + k, nrow), col),
            device_id_type=pl.DeviceIdType.MESH,
        )
    for k in range(1, ncol):
        pl.semaphore_signal(
            barrier,
            inc=1,
            device_id=(row, lax.rem(col + k, ncol)),
            device_id_type=pl.DeviceIdType.MESH,
        )
    pl.semaphore_wait(barrier, nrow + ncol - 2)


def gather_kernel(
    nrow, ncol, tok, rts, low, out, rts_out, low_out,
    own_sem, z_send, z_recv, g_send, g_recv, pair_send, pass_send, r_send, r_recv, l_send, l_recv,
):
    row, col = lax.axis_index("row"), lax.axis_index("col")
    pair = col + 1 - 2 * lax.rem(col, 2)
    width = tok.shape[1]
    half = ncol // 2

    def block(group, part):
        return out.at[group, :, pl.ds(pl.multiple_of(part * width, width), width)]

    greet(nrow, ncol, row, col)
    own = [
        pltpu.make_async_copy(tok, block(col, row), own_sem.at[0]),
        pltpu.make_async_copy(rts, rts_out.at[col], own_sem.at[1]),
        pltpu.make_async_copy(low, low_out.at[row], own_sem.at[2]),
    ]
    sent = []

    def go(copy):
        copy.start()
        sent.append(copy)

    for k in range(1, nrow):
        there = lax.rem(row + k, nrow)
        go(remote(tok, block(col, row), z_send.at[k], z_recv.at[row], there, col))
    for k in range(nrow):
        part = lax.rem(row + k, nrow)
        if k:
            remote(
                block(col, part), block(col, part), z_send.at[k], z_recv.at[part], row, pair
            ).wait_recv()
        src = tok if k == 0 else block(col, part)
        for m in range(1, half):
            there = lax.rem(col + 2 * m, ncol)
            go(remote(src, block(col, part), g_send.at[k, m], g_recv.at[col, part], row, there))
        go(remote(src, block(col, part), pair_send.at[k], g_recv.at[col, part], row, pair))
        if k == 0:
            for copy in own:
                copy.start()
            for j in range(1, nrow):
                there = lax.rem(row + j, nrow)
                go(remote(low, low_out.at[row], l_send.at[j], l_recv.at[row], there, col))
            for j in range(1, ncol):
                there = lax.rem(col + j, ncol)
                go(remote(rts, rts_out.at[col], r_send.at[j], r_recv.at[col], row, there))
    for k in range(nrow):
        part = lax.rem(row + k, nrow)
        for m in range(1, half):
            group = lax.rem(col + ncol - 2 * m, ncol)
            copy = remote(
                block(group, part), block(group, part), pass_send.at[k, m], g_recv.at[group, part], row, pair
            )
            copy.wait_recv()
            go(copy)
    for k in range(nrow):
        part = lax.rem(row + k, nrow)
        for m in range(half):
            group = lax.rem(pair + ncol - 2 * m, ncol)
            remote(
                block(group, part), block(group, part), pass_send.at[k, m], g_recv.at[group, part], row, pair
            ).wait_recv()
    for j in range(1, nrow):
        there = lax.rem(row + j, nrow)
        remote(low, low_out.at[there], l_send.at[j], l_recv.at[there], there, col).wait_recv()
    for j in range(1, ncol):
        there = lax.rem(col + j, ncol)
        remote(rts, rts_out.at[there], r_send.at[j], r_recv.at[there], row, there).wait_recv()
    for copy in own:
        copy.wait()
    for copy in sent:
        copy.wait_send()


def gather_tokens(tokens, routes_t, low_t):
    nrow, ncol = lax.axis_size("row"), lax.axis_size("col")
    count, width = tokens.shape
    half = ncol // 2
    dma = pltpu.SemaphoreType.DMA
    return pl.pallas_call(
        functools.partial(gather_kernel, nrow, ncol),
        out_shape=(
            jax.ShapeDtypeStruct((ncol, count, nrow * width), tokens.dtype),
            jax.ShapeDtypeStruct((ncol, *routes_t.shape), routes_t.dtype),
            jax.ShapeDtypeStruct((nrow, *low_t.shape), low_t.dtype),
        ),
        in_specs=[pl.BlockSpec(memory_space=pl.ANY)] * 3,
        out_specs=(pl.BlockSpec(memory_space=pl.ANY),) * 3,
        scratch_shapes=[
            dma((3,)), dma((nrow,)), dma((nrow,)), dma((nrow, half)), dma((ncol, nrow)), dma((nrow,)),
            dma((nrow, half)), dma((ncol,)), dma((ncol,)), dma((nrow,)), dma((nrow,)),
        ],
        compiler_params=pltpu.CompilerParams(collective_id=0, has_side_effects=True),
        cost_estimate=pl.CostEstimate(
            flops=0, bytes_accessed=20 * ncol * count * width * nrow, transcendentals=0
        ),
        name="gather_tokens",
    )(tokens, routes_t, low_t)


def on_device(
    tokens,
    router,
    shared_gate_vector,
    shared_gate_weight,
    shared_up_weight,
    shared_down_weight,
    routed_gate_weight,
    routed_up_weight,
    routed_down_weight,
    adapter_input_factor,
    adapter_output_factor,
    routes,
    lengths,
    prompt_adapter_index,
    active_adapter_index,
):
    token_count, local_width = tokens.shape
    col_count = lax.axis_size("col")
    col = lax.axis_index("col")
    local_experts = routed_gate_weight.shape[0]
    expert_count = local_experts * col_count
    route_count = routes.shape[1]
    capacity = 2 * token_count * route_count // expert_count
    adapter_count, rank, _ = adapter_input_factor.shape
    request_count = lengths.shape[1]

    gate_full = lax.all_gather(shared_gate_weight, "col", axis=0, tiled=True)
    up_full = lax.all_gather(shared_up_weight, "col", axis=0, tiled=True)
    down_full = lax.all_gather(shared_down_weight, "col", axis=1, tiled=True)

    steps = jnp.arange(request_count, dtype=jnp.int32)
    ends = jnp.sum(jnp.where(steps[:, None] <= steps[None, :], lengths[0][:, None], 0), axis=0)
    position = jnp.arange(token_count, dtype=jnp.int32)
    request_of = jnp.sum((position[:, None] >= ends[None, :]).astype(jnp.int32), axis=1)
    adapter_of_request = jnp.sum(
        jnp.where(
            prompt_adapter_index[0][:, None] == jnp.arange(active_adapter_index.shape[0])[None, :],
            active_adapter_index[None, :],
            0,
        ),
        axis=1,
    )
    adapter_of = jnp.sum(
        jnp.where(request_of[:, None] == steps[None, :], adapter_of_request[None, :], 0), axis=1
    )
    owner = jnp.arange(adapter_count * rank, dtype=jnp.int32) // rank
    mask = adapter_of[:, None] == owner[None, :]
    low_part = lax.dot_general(
        tokens,
        adapter_input_factor.reshape(adapter_count * rank, local_width),
        (((1,), (1,)), ((), ())),
        preferred_element_type=F32,
    )
    low_own = jnp.sum(
        jnp.where(mask, low_part, 0.0).reshape(token_count, adapter_count, rank), axis=1
    )
    routes_t = jnp.pad(routes.T, ((0, 8 - route_count), (0, 0)), constant_values=-1)
    all_tokens, all_routes_t, low_all = gather_tokens(tokens, routes_t, low_own.T)
    all_features = lax.dynamic_index_in_dim(all_tokens, col, 0, keepdims=False)
    full_width = all_features.shape[1]
    low = jnp.sum(low_all, axis=0).T.astype(BF)
    low_masked = jnp.where(mask, jnp.tile(low, (1, adapter_count)), jnp.zeros((), BF))
    delta = dot(
        low_masked, adapter_output_factor.reshape(adapter_count * rank, adapter_output_factor.shape[2])
    )

    logits = dot(all_features, router)
    experts = jnp.arange(expert_count, dtype=jnp.int32)
    onehot = routes[:, :, None] == experts[None, None, :]
    picked = jnp.sum(jnp.where(onehot, logits[:, None, :], 0.0), axis=2)
    raw_exp = jnp.exp(picked)
    gate_weights = raw_exp / jnp.sum(raw_exp, axis=1, keepdims=True)
    share = jax.nn.sigmoid(dot(all_features, shared_gate_vector))
    tri = (position[None, :] < position[:, None]).astype(BF)
    hit = jnp.any(onehot, axis=1)
    rank_own = dot(tri, hit.astype(BF)).astype(jnp.int32)
    weight_of = jnp.sum(jnp.where(onehot, gate_weights[:, :, None], 0.0), axis=1)
    slots = jnp.arange(capacity, dtype=jnp.int32)
    here = hit[:, :, None] & (rank_own[:, :, None] == slots[None, None, :])
    combine = jnp.where(here, weight_of[:, :, None], 0.0).reshape(token_count, expert_count * capacity)
    combine_hi = combine.astype(BF)
    combine_lo = (combine - combine_hi.astype(F32)).astype(BF)

    own_experts = col * local_experts + jnp.arange(local_experts, dtype=jnp.int32)
    hit_all = jnp.any(all_routes_t[:, :, :, None] == own_experts[None, None, None, :], axis=1)
    rank_all = jnp.einsum(
        "ts,gse->gte", tri, hit_all.astype(BF), preferred_element_type=F32
    ).astype(jnp.int32)
    pick = (
        (hit_all[:, :, :, None] & (rank_all[:, :, :, None] == slots[None, None, None, :]))
        .astype(BF)
        .transpose(2, 0, 3, 1)
    )
    rows = jnp.einsum("egst,gtd->egsd", pick, all_tokens, preferred_element_type=F32).astype(BF)
    rows = rows.reshape(local_experts, col_count * capacity, full_width)
    gate_part = jnp.einsum("esd,edf->esf", rows, routed_gate_weight, preferred_element_type=F32)
    up_part = jnp.einsum("esd,edf->esf", rows, routed_up_weight, preferred_element_type=F32)
    hidden = (jax.nn.silu(gate_part) * up_part).astype(BF)
    partial = jnp.einsum(
        "esf,efd->esd", hidden, routed_down_weight, preferred_element_type=F32
    ).astype(BF)
    outgoing = partial.reshape(local_experts, col_count, capacity, full_width).transpose(1, 0, 2, 3)
    returned = lax.all_to_all(outgoing, "col", split_axis=0, concat_axis=0, tiled=True)
    flat = returned.reshape(expert_count * capacity, full_width)

    shared_gate_value = dot(all_features, gate_full)
    shared_up_value = dot(all_features, up_full)
    shared_hidden = (
        jax.nn.silu(shared_gate_value) * (shared_up_value + ADAPTER_SCALE * delta)
    ).astype(BF)
    shared_part = dot(shared_hidden, down_full) * share[:, None]

    total = dot(combine_hi, flat) + dot(combine_lo, flat) + shared_part
    return lax.psum_scatter(total, "row", scatter_dimension=1, tiled=True)


def solution(mesh):
    return jax.shard_map(
        on_device,
        mesh=mesh,
        in_specs=(
            P("col", "row"),
            P(),
            P(),
            P("col", "row"),
            P("col", "row"),
            P("row", "col"),
            P("col", None, "row"),
            P("col", None, "row"),
            P("col", "row", None),
            P(None, None, "row"),
            P(None, None, "row"),
            P("col", None),
            P("col", None),
            P("col", None),
            P(),
        ),
        out_specs=P("col", "row"),
        check_vma=False,
    )
```

```python
import functools

import jax
import jax.numpy as jnp
from jax import lax
from jax.experimental import pallas as pl
from jax.experimental.pallas import tpu as pltpu
from jax.sharding import PartitionSpec as P

ADAPTER_SCALE = 2.0
BF = jnp.bfloat16
F32 = jnp.float32


def dot(a, b):
    return jnp.dot(a, b, preferred_element_type=F32)


def remote(src, dst, send, recv, row, col):
    return pltpu.make_async_remote_copy(
        src_ref=src,
        dst_ref=dst,
        send_sem=send,
        recv_sem=recv,
        device_id=(row, col),
        device_id_type=pl.DeviceIdType.MESH,
    )


def greet(nrow, ncol, row, col):
    barrier = pltpu.get_barrier_semaphore()
    for k in range(1, nrow):
        pl.semaphore_signal(
            barrier,
            inc=1,
            device_id=(lax.rem(row + k, nrow), col),
            device_id_type=pl.DeviceIdType.MESH,
        )
    for k in range(1, ncol):
        pl.semaphore_signal(
            barrier,
            inc=1,
            device_id=(row, lax.rem(col + k, ncol)),
            device_id_type=pl.DeviceIdType.MESH,
        )
    pl.semaphore_wait(barrier, nrow + ncol - 2)


def gather_kernel(
    nrow, ncol, tok, rts, low, out, rts_out, low_out,
    own_sem, z_send, z_recv, g_send, g_recv, pair_send, pass_send, r_send, r_recv, l_send, l_recv,
):
    row, col = lax.axis_index("row"), lax.axis_index("col")
    pair = col + 1 - 2 * lax.rem(col, 2)
    width = tok.shape[1]
    half = ncol // 2

    def block(group, part):
        return out.at[group, :, pl.ds(pl.multiple_of(part * width, width), width)]

    greet(nrow, ncol, row, col)
    own = [
        pltpu.make_async_copy(tok, block(col, row), own_sem.at[0]),
        pltpu.make_async_copy(rts, rts_out.at[col], own_sem.at[1]),
        pltpu.make_async_copy(low, low_out.at[row], own_sem.at[2]),
    ]
    sent = []

    def go(copy):
        copy.start()
        sent.append(copy)

    for k in range(1, nrow):
        there = lax.rem(row + k, nrow)
        go(remote(tok, block(col, row), z_send.at[k], z_recv.at[row], there, col))
    for k in range(nrow):
        part = lax.rem(row + k, nrow)
        if k:
            remote(
                block(col, part), block(col, part), z_send.at[k], z_recv.at[part], row, pair
            ).wait_recv()
        src = tok if k == 0 else block(col, part)
        for m in range(1, half):
            there = lax.rem(col + 2 * m, ncol)
            go(remote(src, block(col, part), g_send.at[k, m], g_recv.at[col, part], row, there))
        go(remote(src, block(col, part), pair_send.at[k], g_recv.at[col, part], row, pair))
        if k == 0:
            for copy in own:
                copy.start()
            for j in range(1, nrow):
                there = lax.rem(row + j, nrow)
                go(remote(low, low_out.at[row], l_send.at[j], l_recv.at[row], there, col))
            for j in range(1, ncol):
                there = lax.rem(col + j, ncol)
                go(remote(rts, rts_out.at[col], r_send.at[j], r_recv.at[col], row, there))
    for k in range(nrow):
        part = lax.rem(row + k, nrow)
        for m in range(1, half):
            group = lax.rem(col + ncol - 2 * m, ncol)
            copy = remote(
                block(group, part), block(group, part), pass_send.at[k, m], g_recv.at[group, part], row, pair
            )
            copy.wait_recv()
            go(copy)
    for k in range(nrow):
        part = lax.rem(row + k, nrow)
        for m in range(half):
            group = lax.rem(pair + ncol - 2 * m, ncol)
            remote(
                block(group, part), block(group, part), pass_send.at[k, m], g_recv.at[group, part], row, pair
            ).wait_recv()
    for j in range(1, nrow):
        there = lax.rem(row + j, nrow)
        remote(low, low_out.at[there], l_send.at[j], l_recv.at[there], there, col).wait_recv()
    for j in range(1, ncol):
        there = lax.rem(col + j, ncol)
        remote(rts, rts_out.at[there], r_send.at[j], r_recv.at[there], row, there).wait_recv()
    for copy in own:
        copy.wait()
    for copy in sent:
        copy.wait_send()


def gather_tokens(tokens, routes_t, low_t):
    nrow, ncol = lax.axis_size("row"), lax.axis_size("col")
    count, width = tokens.shape
    half = ncol // 2
    dma = pltpu.SemaphoreType.DMA
    return pl.pallas_call(
        functools.partial(gather_kernel, nrow, ncol),
        out_shape=(
            jax.ShapeDtypeStruct((ncol, count, nrow * width), tokens.dtype),
            jax.ShapeDtypeStruct((ncol, *routes_t.shape), routes_t.dtype),
            jax.ShapeDtypeStruct((nrow, *low_t.shape), low_t.dtype),
        ),
        in_specs=[pl.BlockSpec(memory_space=pl.ANY)] * 3,
        out_specs=(pl.BlockSpec(memory_space=pl.ANY),) * 3,
        scratch_shapes=[
            dma((3,)), dma((nrow,)), dma((nrow,)), dma((nrow, half)), dma((ncol, nrow)), dma((nrow,)),
            dma((nrow, half)), dma((ncol,)), dma((ncol,)), dma((nrow,)), dma((nrow,)),
        ],
        compiler_params=pltpu.CompilerParams(collective_id=0, has_side_effects=True),
        cost_estimate=pl.CostEstimate(
            flops=0, bytes_accessed=20 * ncol * count * width * nrow, transcendentals=0
        ),
        name="gather_tokens",
    )(tokens, routes_t, low_t)


def row_kernel(nrow, total, out, own_sem, send, recv):
    row, col = lax.axis_index("row"), lax.axis_index("col")
    width = out.shape[2]
    greet(nrow, 1, row, col)

    def part(there):
        return total.at[:, pl.ds(pl.multiple_of(there * width, width), width)]

    copies = []
    for k in range(1, nrow):
        there = lax.rem(row + k, nrow)
        copies.append(remote(part(there), out.at[row], send.at[k], recv.at[row], there, col))
        copies[-1].start()
    own = pltpu.make_async_copy(part(row), out.at[row], own_sem)
    own.start()
    own.wait()
    for k in range(1, nrow):
        there = lax.rem(row + k, nrow)
        remote(part(there), out.at[there], send.at[k], recv.at[there], there, col).wait_recv()
    for copy in copies:
        copy.wait_send()


def exchange_rows(total, width):
    nrow = lax.axis_size("row")
    dma = pltpu.SemaphoreType.DMA
    return pl.pallas_call(
        functools.partial(row_kernel, nrow),
        out_shape=jax.ShapeDtypeStruct((nrow, total.shape[0], width), total.dtype),
        in_specs=[pl.BlockSpec(memory_space=pl.ANY)],
        out_specs=pl.BlockSpec(memory_space=pl.ANY),
        scratch_shapes=[dma, dma((nrow,)), dma((nrow,))],
        compiler_params=pltpu.CompilerParams(collective_id=1, has_side_effects=True),
        name="exchange_rows",
    )(total)


def on_device(
    tokens,
    router,
    shared_gate_vector,
    shared_gate_weight,
    shared_up_weight,
    shared_down_weight,
    routed_gate_weight,
    routed_up_weight,
    routed_down_weight,
    adapter_input_factor,
    adapter_output_factor,
    routes,
    lengths,
    prompt_adapter_index,
    active_adapter_index,
):
    token_count, local_width = tokens.shape
    col_count = lax.axis_size("col")
    col = lax.axis_index("col")
    local_experts = routed_gate_weight.shape[0]
    expert_count = local_experts * col_count
    route_count = routes.shape[1]
    capacity = 2 * token_count * route_count // expert_count
    adapter_count, rank, _ = adapter_input_factor.shape
    request_count = lengths.shape[1]

    gate_full = lax.all_gather(shared_gate_weight, "col", axis=0, tiled=True)
    up_full = lax.all_gather(shared_up_weight, "col", axis=0, tiled=True)
    down_full = lax.all_gather(shared_down_weight, "col", axis=1, tiled=True)

    steps = jnp.arange(request_count, dtype=jnp.int32)
    ends = jnp.sum(jnp.where(steps[:, None] <= steps[None, :], lengths[0][:, None], 0), axis=0)
    position = jnp.arange(token_count, dtype=jnp.int32)
    request_of = jnp.sum((position[:, None] >= ends[None, :]).astype(jnp.int32), axis=1)
    adapter_of_request = jnp.sum(
        jnp.where(
            prompt_adapter_index[0][:, None] == jnp.arange(active_adapter_index.shape[0])[None, :],
            active_adapter_index[None, :],
            0,
        ),
        axis=1,
    )
    adapter_of = jnp.sum(
        jnp.where(request_of[:, None] == steps[None, :], adapter_of_request[None, :], 0), axis=1
    )
    owner = jnp.arange(adapter_count * rank, dtype=jnp.int32) // rank
    mask = adapter_of[:, None] == owner[None, :]
    low_part = lax.dot_general(
        tokens,
        adapter_input_factor.reshape(adapter_count * rank, local_width),
        (((1,), (1,)), ((), ())),
        preferred_element_type=F32,
    )
    low_own = jnp.sum(
        jnp.where(mask, low_part, 0.0).reshape(token_count, adapter_count, rank), axis=1
    )
    routes_t = jnp.pad(routes.T, ((0, 8 - route_count), (0, 0)), constant_values=-1)
    all_tokens, all_routes_t, low_all = gather_tokens(tokens, routes_t, low_own.T)
    all_features = lax.dynamic_index_in_dim(all_tokens, col, 0, keepdims=False)
    full_width = all_features.shape[1]
    low = jnp.sum(low_all, axis=0).T.astype(BF)
    low_masked = jnp.where(mask, jnp.tile(low, (1, adapter_count)), jnp.zeros((), BF))
    delta = dot(
        low_masked, adapter_output_factor.reshape(adapter_count * rank, adapter_output_factor.shape[2])
    )

    logits = dot(all_features, router)
    experts = jnp.arange(expert_count, dtype=jnp.int32)
    onehot = routes[:, :, None] == experts[None, None, :]
    picked = jnp.sum(jnp.where(onehot, logits[:, None, :], 0.0), axis=2)
    raw_exp = jnp.exp(picked)
    gate_weights = raw_exp / jnp.sum(raw_exp, axis=1, keepdims=True)
    share = jax.nn.sigmoid(dot(all_features, shared_gate_vector))
    tri = (position[None, :] < position[:, None]).astype(BF)
    hit = jnp.any(onehot, axis=1)
    rank_own = dot(tri, hit.astype(BF)).astype(jnp.int32)
    weight_of = jnp.sum(jnp.where(onehot, gate_weights[:, :, None], 0.0), axis=1)
    slots = jnp.arange(capacity, dtype=jnp.int32)
    here = hit[:, :, None] & (rank_own[:, :, None] == slots[None, None, :])
    combine = jnp.where(here, weight_of[:, :, None], 0.0).reshape(
        token_count, col_count, local_experts, capacity
    )
    combine_hi = combine.astype(BF)
    combine_lo = (combine - combine_hi.astype(F32)).astype(BF)

    own_experts = col * local_experts + jnp.arange(local_experts, dtype=jnp.int32)
    hit_all = jnp.any(all_routes_t[:, :, :, None] == own_experts[None, None, None, :], axis=1)
    rank_all = jnp.einsum(
        "ts,gse->gte", tri, hit_all.astype(BF), preferred_element_type=F32
    ).astype(jnp.int32)
    pick = (
        (hit_all[:, :, :, None] & (rank_all[:, :, :, None] == slots[None, None, None, :]))
        .astype(BF)
        .transpose(2, 0, 3, 1)
    )
    flats = []
    for e in range(local_experts):
        rows = jnp.einsum("gst,gtd->gsd", pick[e], all_tokens, preferred_element_type=F32)
        rows = rows.astype(BF).reshape(col_count * capacity, full_width)
        gate_part = dot(rows, routed_gate_weight[e])
        up_part = dot(rows, routed_up_weight[e])
        hidden = (jax.nn.silu(gate_part) * up_part).astype(BF)
        partial = dot(hidden, routed_down_weight[e]).astype(BF)
        outgoing = partial.reshape(col_count, capacity, full_width)
        returned = lax.all_to_all(outgoing, "col", split_axis=0, concat_axis=0, tiled=True)
        flats.append(returned.reshape(col_count * capacity, full_width))

    shared_gate_value = dot(all_features, gate_full)
    shared_up_value = dot(all_features, up_full)
    shared_hidden = (
        jax.nn.silu(shared_gate_value) * (shared_up_value + ADAPTER_SCALE * delta)
    ).astype(BF)
    shared_hidden, combine_hi, combine_lo = lax.optimization_barrier(
        (shared_hidden, combine_hi, combine_lo)
    )
    total = dot(shared_hidden, down_full) * share[:, None]
    for e in range(local_experts):
        for part in (combine_hi, combine_lo):
            total = total + dot(part[:, :, e].reshape(token_count, col_count * capacity), flats[e])
    return jnp.sum(exchange_rows(total.astype(BF), local_width).astype(F32), axis=0)


def solution(mesh):
    return jax.shard_map(
        on_device,
        mesh=mesh,
        in_specs=(
            P("col", "row"),
            P(),
            P(),
            P("col", "row"),
            P("col", "row"),
            P("row", "col"),
            P("col", None, "row"),
            P("col", None, "row"),
            P("col", "row", None),
            P(None, None, "row"),
            P(None, None, "row"),
            P("col", None),
            P("col", None),
            P("col", None),
            P(),
        ),
        out_specs=P("col", "row"),
        check_vma=False,
    )
```
